32 devices in a mesh: grp: 2 (over y), wide: 8 (over z, x), tp: 2 (over core).
Axes of the slice: x: 2, y: 2, z: 4, core: 2. Of those that a mesh axis runs over, the one named last changes fastest.
Arguments:
- hidden: bfloat16 [64, 4096], P(('grp', 'wide')), parts along dimension 0, may hold values from -6 to 6
- residual: bfloat16 [64, 4096], P(('grp', 'wide'), 'tp'), parts along dimension 0, may hold values from -6 to 6
- output_weight: bfloat16 [4096, 4096], P('wide', 'tp'), may hold values from -0.09375 to 0.09375
- adapter_down_factor: bfloat16 [64, 64, 4096], P('wide', None, 'tp'), may hold values from -0.09375 to 0.09375
- adapter_up_factor: bfloat16 [64, 64, 4096], P('wide', None, 'tp'), may hold values from -0.75 to 0.75
- gain: float32 [4096], P('tp'), may hold values from 0.4 to 1.6
- block_request_rows: int32 [32, 4], P(('grp', 'wide')), parts along dimension 0, may hold values from 0 to 32, as said below
- adapter_of_block: int32 [32], P(('grp', 'wide')), parts along dimension 0, may hold values from 0 to 63, as said below
Outputs:
- new_residual: bfloat16 [64, 4096], P(('grp', 'wide'), 'tp'), parts along dimension 0
- normed: bfloat16 [64, 4096], P(('grp', 'wide'), 'tp'), parts along dimension 0
The draws below stay inside these ranges and needn't reach their ends.
There are 2 independent parts, one for each index of `grp`. The reference program is written for one: setup_inputs(seed, part) draws one part's arguments, and reference() takes and returns one part's arrays. A program takes and returns all parts, laid end to end along the dimension named above; an argument that names none is the same for every part. Nothing has to cross between parts.
Inputs may be any that keep to these rules, and one draw needn't show every extreme that they name: `block_request_rows`: each request index of 0 to 31 stands in exactly one slot; unused slots hold 32 and follow the used ones in their row; some block is full and some is empty. `adapter_of_block`: block b names an adapter held by the same index of wide: between (b // 2) * 8 and that plus 8 - 1; an adapter may have several blocks or none.
All inputs are finite; a program needn't handle non-finite values.
Results may differ from the reference program's by a relative error of at most 0.0033.
Values may be sent and summed in bfloat16 or wider, within the bound.
No kernel may reach another device: no remote copies, remote signals or barrier semaphores. Data moves between devices by JAX's collectives and lax.ppermute only.
A program may use at most 64 MiB of HBM per device.

```python
import jax
import jax.numpy as jnp
from jax import lax

MODEL_WIDTH = 4096
ADAPTER_RANK = 64
ADP_DEV = 8
BLK = 4
ACT_DEV = 2
REQ = 32
ADAPTER_TOTAL = 64


def draw_block_request_rows(key, part):
    key = jax.random.fold_in(key, 7)
    key_order, key_counts = jax.random.split(key, 2)
    blocks = 2 * REQ // BLK
    half_blocks = blocks // 2
    first = jax.random.randint(key_counts, (half_blocks,), 0, BLK + 1).astype(jnp.int32)
    first = first.at[0].set(BLK)
    counts = jnp.concatenate([first, BLK - first], axis=0)
    starts = jnp.cumsum(counts) - counts
    order = jax.random.permutation(key_order, REQ).astype(jnp.int32)
    slot_index = jnp.arange(BLK, dtype=jnp.int32)
    position = starts[:, None] + slot_index[None, :]
    valid = slot_index[None, :] < counts[:, None]
    position = jnp.minimum(position, REQ - 1)
    table = jnp.where(valid, jnp.take(order, position), REQ)
    return table.astype(jnp.int32)


def draw_adapter_of_block(key, part):
    key = jax.random.fold_in(key, 11)
    blocks = 2 * REQ // BLK
    block_index = jnp.arange(blocks, dtype=jnp.int32)
    owner = block_index // ACT_DEV
    local_pick = jax.random.randint(key, (blocks,), 0, ADP_DEV).astype(jnp.int32)
    local_pick = local_pick.at[0].set(0)
    local_pick = local_pick.at[blocks - 1].set(ADP_DEV - 1)
    return (owner * ADP_DEV + local_pick).astype(jnp.int32)


def shard_levels(stream_key, shape, shards, low, largest):
    level, own = 1.0, jax.random.fold_in(stream_key, 6)
    for dim, parts in shards:
        draws = jnp.exp(jax.random.uniform(jax.random.fold_in(own, dim), (parts,), jnp.float32, low / len(shards), largest / len(shards)))
        level = level * jnp.repeat(draws, shape[dim] // parts).reshape([-1 if axis == dim else 1 for axis in range(len(shape))])
    return level


def scatter_about(key, extent, deviation, most, pieces=(), held_as=jnp.bfloat16):
    level = shard_levels(key, extent, pieces, -0.22, 0.18) if pieces else 1.0
    drawn = jax.random.normal(key, extent, jnp.float32) * deviation * level
    return jnp.minimum(jnp.maximum(drawn, -most), most).astype(held_as)


def setup_inputs(seed: int = 0, part: int = 0) -> dict:
    splits = jax.random.split(jax.random.key(seed), 9)
    own_keys = jax.random.split(jax.random.fold_in(splits[8], part), 9)
    hidden = scatter_about(own_keys[0], (REQ, MODEL_WIDTH), 1.0, 6.0, ((0, 8),))
    residual = scatter_about(own_keys[1], (REQ, MODEL_WIDTH), 1.0, 6.0, ((0, 8), (1, 2)))
    output_weight = scatter_about(splits[2], (MODEL_WIDTH, MODEL_WIDTH), MODEL_WIDTH ** -0.5, 0.09375, ((0, 8), (1, 2)))
    adapter_down_factor = scatter_about(splits[3], (ADAPTER_TOTAL, ADAPTER_RANK, MODEL_WIDTH), MODEL_WIDTH ** -0.5, 0.09375, ((0, 8), (2, 2)))
    adapter_up_factor = scatter_about(splits[4], (ADAPTER_TOTAL, ADAPTER_RANK, MODEL_WIDTH), ADAPTER_RANK ** -0.5, 0.75, ((0, 8), (2, 2)))
    gain = jnp.clip(1.0 + 0.12 * jax.random.normal(splits[5], (MODEL_WIDTH,), jnp.float32), 0.4, 1.6)
    block_request_rows = draw_block_request_rows(jax.random.fold_in(jax.random.fold_in(splits[8], part), 71), part)
    adapter_of_block = draw_adapter_of_block(jax.random.fold_in(jax.random.fold_in(splits[8], part), 71), part)
    return dict(hidden=hidden, residual=residual, output_weight=output_weight, adapter_down_factor=adapter_down_factor, adapter_up_factor=adapter_up_factor, gain=gain, block_request_rows=block_request_rows, adapter_of_block=adapter_of_block)


epsilon = 1e-06

def reference(hidden, residual, output_weight, adapter_down_factor, adapter_up_factor, gain, block_request_rows, adapter_of_block):
    projected = jnp.dot(hidden, output_weight, preferred_element_type=jnp.float32)
    padded_rows = jnp.concatenate([hidden, jnp.zeros((1, hidden.shape[1]), hidden.dtype)], axis=0)
    picked = jnp.take(padded_rows, block_request_rows, axis=0)
    selected_down = jnp.take(adapter_down_factor, adapter_of_block, axis=0)
    selected_up = jnp.take(adapter_up_factor, adapter_of_block, axis=0)
    inner = jnp.einsum('bsd,brd->bsr', picked.astype(jnp.float32), selected_down.astype(jnp.float32)).astype(jnp.bfloat16)
    update_term = jnp.einsum('bsr,brd->bsd', inner.astype(jnp.float32), selected_up.astype(jnp.float32))
    combined = projected.at[block_request_rows.reshape(-1)].add(update_term.reshape(-1, hidden.shape[1]), mode='drop')
    summed = residual.astype(jnp.float32) + combined
    mean_square = lax.optimization_barrier(jnp.mean(summed * summed, axis=1, keepdims=True))
    normed = summed * lax.rsqrt(mean_square + epsilon) * gain
    return (summed.astype(jnp.bfloat16), normed.astype(jnp.bfloat16))
```

```python
import jax
import jax.numpy as jnp
from jax import lax
from jax.sharding import PartitionSpec as P

epsilon = 1e-06


def local(
    hidden,
    residual,
    output_weight,
    adapter_down_factor,
    adapter_up_factor,
    gain,
    block_request_rows,
    adapter_of_block,
):
    rows, width = hidden.shape
    half_width = residual.shape[1]
    wide = lax.axis_size("wide")
    requests = wide * rows
    feature_count = output_weight.shape[0]
    adapters_here, rank, _ = adapter_down_factor.shape
    blocks = adapter_of_block.shape[0]
    core = lax.axis_index("tp")
    swap = [(0, 1), (1, 0)]

    ids = adapter_of_block - lax.axis_index("wide") * adapters_here
    selected_down = jnp.take(adapter_down_factor, ids, axis=0, mode="clip").reshape(blocks * rank, half_width)
    selected_up = jnp.take(adapter_up_factor, ids, axis=0, mode="clip").reshape(blocks * rank, half_width)

    half = lax.dynamic_slice_in_dim(hidden, core * half_width, half_width, 1)
    columns = hidden.reshape(rows, wide, feature_count).transpose(1, 0, 2)
    sent = jnp.concatenate(
        [jnp.broadcast_to(half[None], (wide, rows, half_width)), columns], axis=2
    )
    received = lax.all_to_all(sent, "wide", 0, 0).reshape(requests, half_width + feature_count)
    half_rows = received[:, :half_width]
    own_features = received[:, half_width:]

    inner_part = lax.dot_general(
        half_rows, selected_down, (((1,), (1,)), ((), ())), preferred_element_type=jnp.float32
    )
    inner_other = lax.ppermute(inner_part, "tp", swap)
    inner = (inner_part + inner_other).astype(jnp.bfloat16)
    request_index = lax.broadcasted_iota(jnp.int32, (requests, blocks), 0)
    holds = jnp.any(request_index[:, :, None] == block_request_rows[None], axis=2)
    inner = jnp.where(jnp.repeat(holds, rank, axis=1), inner, jnp.zeros_like(inner))

    partial_value = jnp.dot(own_features, output_weight, preferred_element_type=jnp.float32)
    partial_value += jnp.dot(inner, selected_up, preferred_element_type=jnp.float32)
    terms = lax.all_to_all(
        partial_value.astype(jnp.bfloat16).reshape(wide, rows, half_width), "wide", 0, 0
    )
    summed = residual.astype(jnp.float32) + jnp.sum(terms.astype(jnp.float32), axis=0)
    squares = jnp.sum(summed * summed, axis=1, keepdims=True)
    squares += lax.ppermute(squares, "tp", swap)
    normed = summed * lax.rsqrt(squares / width + epsilon) * gain
    return (summed.astype(jnp.bfloat16), normed.astype(jnp.bfloat16))


def solution(mesh):
    return jax.shard_map(
        local,
        mesh=mesh,
        in_specs=(
            P(("grp", "wide"), None),
            P(("grp", "wide"), "tp"),
            P("wide", "tp"),
            P("wide", None, "tp"),
            P("wide", None, "tp"),
            P("tp"),
            P(("grp", "wide"), None),
            P(("grp", "wide")),
        ),
        out_specs=(P(("grp", "wide"), "tp"), P(("grp", "wide"), "tp")),
        check_vma=False,
    )
```

```python
import functools

import jax
import jax.numpy as jnp
from jax import lax
from jax.experimental import pallas as pl
from jax.experimental.pallas import tpu as pltpu
from jax.sharding import PartitionSpec as P

epsilon = 1e-06
VMEM = pl.BlockSpec(memory_space=pltpu.VMEM)
SMEM = pl.BlockSpec(memory_space=pltpu.SMEM)
ANY = pl.BlockSpec(memory_space=pl.ANY)


def exchange_order(wide):
    if wide == 8:
        return [4, 1, 0, 3, 7, 2, 5, 6]
    middle = wide // 2
    return [middle] + [index for index in range(wide) if index != middle]


def pack(order, half_width, feature_count, hidden_ref, sent_ref):
    start = pl.multiple_of(lax.axis_index("tp") * half_width, 128)
    half = hidden_ref[:, pl.ds(start, half_width)]
    for place, device in enumerate(order):
        sent_ref[place, :, :half_width] = half
        sent_ref[place, :, half_width:] = hidden_ref[
            :, device * feature_count : (device + 1) * feature_count
        ]


def fetch(
    order, rows, adapters_here, ids_ref, slots_ref, down_ref, up_ref, down_out, up_out, holds_out, sems
):
    blocks, rank, _ = down_out.shape
    base = lax.axis_index("wide") * adapters_here
    copies = []
    for block in range(blocks):
        adapter = jnp.clip(ids_ref[block] - base, 0, adapters_here - 1)
        copies.append(
            pltpu.make_async_copy(down_ref.at[adapter], down_out.at[block], sems.at[2 * block])
        )
        copies.append(
            pltpu.make_async_copy(up_ref.at[adapter], up_out.at[block], sems.at[2 * block + 1])
        )
    for copy in copies:
        copy.start()
    requests = holds_out.shape[0]
    line = lax.broadcasted_iota(jnp.int32, (requests, rank), 0)
    place, within = line // rows, line % rows
    device = place
    for index, member in enumerate(order):
        if member != index:
            device = jnp.where(place == index, member, device)
    request = device * rows + within
    for block in range(blocks):
        held = request == slots_ref[block, 0]
        for slot in range(1, slots_ref.shape[1]):
            held = held | (request == slots_ref[block, slot])
        holds_out[:, block * rank : (block + 1) * rank] = held.astype(jnp.float32)
    for copy in copies:
        copy.wait()


def local(
    hidden,
    residual,
    output_weight,
    adapter_down_factor,
    adapter_up_factor,
    gain,
    block_request_rows,
    adapter_of_block,
):
    rows, width = hidden.shape
    half_width = residual.shape[1]
    wide = lax.axis_size("wide")
    requests = wide * rows
    feature_count = output_weight.shape[0]
    adapters_here, rank, _ = adapter_down_factor.shape
    blocks = adapter_of_block.shape[0]
    swap = [(0, 1), (1, 0)]
    order = exchange_order(wide)
    exchange = functools.partial(
        lax.all_to_all, axis_name="wide", split_axis=0, concat_axis=0, axis_index_groups=[order]
    )

    sent = pl.pallas_call(
        functools.partial(pack, order, half_width, feature_count),
        out_shape=jax.ShapeDtypeStruct((wide, rows, half_width + feature_count), jnp.bfloat16),
        in_specs=[VMEM],
        out_specs=VMEM,
        name="pack",
    )(hidden)
    received = exchange(sent).reshape(requests, half_width + feature_count)
    half_rows = received[:, :half_width]
    own_features = received[:, half_width:]

    factor = (blocks, rank, half_width)
    selected_down, selected_up, holds = pl.pallas_call(
        functools.partial(fetch, order, rows, adapters_here),
        out_shape=[pltpu.VMEM(factor, jnp.bfloat16)] * 2
        + [pltpu.VMEM((requests, blocks * rank), jnp.float32)],
        in_specs=[SMEM, SMEM, ANY, ANY],
        out_specs=[VMEM, VMEM, VMEM],
        scratch_shapes=[pltpu.SemaphoreType.DMA((2 * blocks,))],
        cost_estimate=pl.CostEstimate(
            flops=0, bytes_accessed=8 * blocks * rank * half_width, transcendentals=0
        ),
        name="fetch",
    )(adapter_of_block, block_request_rows, adapter_down_factor, adapter_up_factor)
    selected_down = selected_down.reshape(blocks * rank, half_width)
    selected_up = selected_up.reshape(blocks * rank, half_width)

    inner_part = lax.dot_general(
        half_rows, selected_down, (((1,), (1,)), ((), ())), preferred_element_type=jnp.float32
    )
    inner_other = lax.ppermute(inner_part, "tp", swap)
    inner = (inner_part + inner_other).astype(jnp.bfloat16)
    inner = jnp.where(holds != 0, inner, jnp.zeros_like(inner))

    partial_value = jnp.dot(own_features, output_weight, preferred_element_type=jnp.float32)
    partial_value += jnp.dot(inner, selected_up, preferred_element_type=jnp.float32)
    terms = exchange(partial_value.astype(jnp.bfloat16).reshape(wide, rows, half_width))
    summed = residual.astype(jnp.float32) + jnp.sum(terms.astype(jnp.float32), axis=0)
    squares = jnp.sum(summed * summed, axis=1, keepdims=True)
    squares += lax.ppermute(squares, "tp", swap)
    normed = summed * lax.rsqrt(squares / width + epsilon) * gain
    return (summed.astype(jnp.bfloat16), normed.astype(jnp.bfloat16))


def solution(mesh):
    return jax.shard_map(
        local,
        mesh=mesh,
        in_specs=(
            P(("grp", "wide"), None),
            P(("grp", "wide"), "tp"),
            P("wide", "tp"),
            P("wide", None, "tp"),
            P("wide", None, "tp"),
            P("tp"),
            P(("grp", "wide"), None),
            P(("grp", "wide")),
        ),
        out_specs=(P(("grp", "wide"), "tp"), P(("grp", "wide"), "tp")),
        check_vma=False,
    )
```

```python
import functools

import jax
import jax.numpy as jnp
from jax import lax
from jax.experimental import pallas as pl
from jax.experimental.pallas import tpu as pltpu
from jax.sharding import PartitionSpec as P

epsilon = 1e-06
VMEM = pl.BlockSpec(memory_space=pltpu.VMEM)
SMEM = pl.BlockSpec(memory_space=pltpu.SMEM)
HBM = pl.BlockSpec(memory_space=pltpu.HBM)


def in_vmem(*arrays):
    return [pltpu.with_memory_space_constraint(array, pltpu.VMEM) for array in arrays]


def in_hbm(*arrays):
    return [pltpu.with_memory_space_constraint(array, pltpu.HBM) for array in arrays]


def exchange_orders(wide):
    if wide == 8:
        return [4, 1, 0, 3, 7, 2, 5, 6], [5, 7, 3, 1, 0, 2, 6, 4]
    middle = wide // 2
    order = [middle] + [index for index in range(wide) if index != middle]
    return order, order


def pack(half_width, hidden_ref, sent_ref):
    start = pl.multiple_of(lax.axis_index("tp") * half_width, 128)
    half = hidden_ref[:, pl.ds(start, half_width)]
    for place in range(sent_ref.shape[0]):
        sent_ref[place] = half


def fetch(
    order,
    rows,
    adapters_here,
    ids_ref,
    slots_ref,
    weight_ref,
    down_ref,
    up_ref,
    weight_out,
    down_out,
    up_out,
    holds_out,
    sems,
):
    blocks, rank, _ = down_out.shape
    base = lax.axis_index("wide") * adapters_here
    copies = [pltpu.make_async_copy(weight_ref, weight_out, sems.at[2 * blocks])]
    for block in range(blocks):
        adapter = jnp.clip(ids_ref[block] - base, 0, adapters_here - 1)
        copies.append(
            pltpu.make_async_copy(down_ref.at[adapter], down_out.at[block], sems.at[2 * block])
        )
        copies.append(
            pltpu.make_async_copy(up_ref.at[adapter], up_out.at[block], sems.at[2 * block + 1])
        )
    for copy in copies:
        copy.start()
    requests = holds_out.shape[0]
    line = lax.broadcasted_iota(jnp.int32, (requests, rank), 0)
    place, within = line // rows, line % rows
    device = place
    for index, member in enumerate(order):
        if member != index:
            device = jnp.where(place == index, member, device)
    request = device * rows + within
    for block in range(blocks):
        held = request == slots_ref[block, 0]
        for slot in range(1, slots_ref.shape[1]):
            held = held | (request == slots_ref[block, slot])
        holds_out[:, block * rank : (block + 1) * rank] = held.astype(jnp.float32)
    for copy in copies:
        copy.wait()


def project(own_columns_ref, other_columns_ref, weight_ref, projected_ref):
    feature_count, half_width = weight_ref.shape
    mine = lax.axis_index("wide") * feature_count // half_width == lax.axis_index("tp")
    columns = jnp.where(mine, own_columns_ref[...], other_columns_ref[...])
    projected_ref[...] = jnp.dot(columns, weight_ref[...], preferred_element_type=jnp.float32)


def combine(
    first, second, rows, projected_ref, own_ref, other_ref, holds_ref, up_ref, sent_ref
):
    inner = (own_ref[...] + other_ref[...]).astype(jnp.bfloat16)
    inner = jnp.where(holds_ref[...] != 0, inner, jnp.zeros_like(inner))
    total = projected_ref[...] + jnp.dot(inner, up_ref[...], preferred_element_type=jnp.float32)
    for place, device in enumerate(second):
        start = first.index(device) * rows
        sent_ref[place] = total[start : start + rows].astype(sent_ref.dtype)


def local(
    hidden,
    residual,
    output_weight,
    adapter_down_factor,
    adapter_up_factor,
    gain,
    block_request_rows,
    adapter_of_block,
):
    rows, width = hidden.shape
    half_width = residual.shape[1]
    wide = lax.axis_size("wide")
    requests = wide * rows
    feature_count = output_weight.shape[0]
    adapters_here, rank, _ = adapter_down_factor.shape
    blocks = adapter_of_block.shape[0]
    swap = [(0, 1), (1, 0)]
    first, second = exchange_orders(wide)

    params = pltpu.CompilerParams(vmem_limit_bytes=16 * 2**20)

    def exchange(order, sent):
        return lax.all_to_all(sent, "wide", 0, 0, axis_index_groups=[order])

    sent = pl.pallas_call(
        functools.partial(pack, half_width),
        out_shape=jax.ShapeDtypeStruct((wide, rows, half_width), jnp.bfloat16),
        in_specs=[VMEM],
        out_specs=VMEM,
        compiler_params=params,
        name="pack",
    )(*in_hbm(hidden))
    half_rows = exchange(first, sent).reshape(requests, half_width)

    factor = (blocks, rank, half_width)
    weight, selected_down, selected_up, holds = pl.pallas_call(
        functools.partial(fetch, first, rows, adapters_here),
        out_shape=[pltpu.VMEM(output_weight.shape, jnp.bfloat16)]
        + [pltpu.VMEM(factor, jnp.bfloat16)] * 2
        + [pltpu.VMEM((requests, blocks * rank), jnp.float32)],
        in_specs=[SMEM, SMEM, HBM, HBM, HBM],
        out_specs=[VMEM] * 4,
        scratch_shapes=[pltpu.SemaphoreType.DMA((2 * blocks + 1,))],
        cost_estimate=pl.CostEstimate(
            flops=0, bytes_accessed=8 * blocks * rank * half_width, transcendentals=0
        ),
        compiler_params=params,
        name="fetch",
    )(
        *in_hbm(
            adapter_of_block,
            block_request_rows,
            output_weight,
            adapter_down_factor,
            adapter_up_factor,
        )
    )
    selected_down = selected_down.reshape(blocks * rank, half_width)
    selected_up = selected_up.reshape(blocks * rank, half_width)

    start = lax.axis_index("wide") * feature_count
    own_columns = lax.dynamic_slice_in_dim(half_rows, start % half_width, feature_count, 1)
    other_columns = lax.ppermute(own_columns, "tp", swap)
    inner_part = lax.dot_general(
        half_rows, selected_down, (((1,), (1,)), ((), ())), preferred_element_type=jnp.float32
    )
    inner_other = lax.ppermute(inner_part, "tp", swap)
    projected = pl.pallas_call(
        project,
        out_shape=pltpu.VMEM((requests, half_width), jnp.float32),
        in_specs=[VMEM] * 3,
        out_specs=VMEM,
        compiler_params=params,
        cost_estimate=pl.CostEstimate(
            flops=2 * requests * feature_count * half_width,
            bytes_accessed=2 * feature_count * half_width + 4 * requests * half_width,
            transcendentals=0,
        ),
        name="project",
    )(*in_vmem(own_columns, other_columns, weight))
    terms = pl.pallas_call(
        functools.partial(combine, first, second, rows),
        out_shape=pltpu.VMEM((wide, rows, half_width), jnp.bfloat16),
        in_specs=[VMEM] * 5,
        out_specs=VMEM,
        compiler_params=params,
        name="combine",
    )(*in_vmem(projected, inner_part, inner_other, holds, selected_up))
    terms = exchange(second, terms)
    summed = residual.astype(jnp.float32) + jnp.sum(terms.astype(jnp.float32), axis=0)
    squares = jnp.sum(summed * summed, axis=1, keepdims=True)
    squares += lax.ppermute(squares, "tp", swap)
    normed = summed * lax.rsqrt(squares / width + epsilon) * gain
    return (summed.astype(jnp.bfloat16), normed.astype(jnp.bfloat16))


def solution(mesh):
    return jax.shard_map(
        local,
        mesh=mesh,
        in_specs=(
            P(("grp", "wide"), None),
            P(("grp", "wide"), "tp"),
            P("wide", "tp"),
            P("wide", None, "tp"),
            P("wide", None, "tp"),
            P("tp"),
            P(("grp", "wide"), None),
            P(("grp", "wide")),
        ),
        out_specs=(P(("grp", "wide"), "tp"), P(("grp", "wide"), "tp")),
        check_vma=False,
    )
```

```python
import functools

import jax
import jax.numpy as jnp
from jax import lax
from jax.experimental import pallas as pl
from jax.experimental.pallas import tpu as pltpu
from jax.sharding import PartitionSpec as P

epsilon = 1e-06
VMEM = pl.BlockSpec(memory_space=pltpu.VMEM)
SMEM = pl.BlockSpec(memory_space=pltpu.SMEM)
HBM = pl.BlockSpec(memory_space=pltpu.HBM)


def in_vmem(*arrays):
    return [pltpu.with_memory_space_constraint(array, pltpu.VMEM) for array in arrays]


def in_hbm(*arrays):
    return [pltpu.with_memory_space_constraint(array, pltpu.HBM) for array in arrays]


def exchange_orders(wide):
    if wide == 8:
        return [3, 2, 7, 0, 1, 6, 4, 5], [4, 6, 0, 7, 5, 1, 2, 3]
    middle = wide // 2
    order = [middle] + [index for index in range(wide) if index != middle]
    return order, order


def core_in_first_group(device, wide):
    return device // (wide // 2)


def pack(order, half_width, hidden_ref, sent_ref):
    wide = sent_ref.shape[0]
    core = lax.axis_index("tp")
    swapped = (core + core_in_first_group(lax.axis_index("wide"), wide)) % 2
    halves = []
    for member_core in range(2):
        start = pl.multiple_of((member_core + swapped) % 2 * half_width, 128)
        halves.append(hidden_ref[:, pl.ds(start, half_width)])
    for place, device in enumerate(order):
        sent_ref[place] = halves[core_in_first_group(device, wide)]


def fetch(
    order,
    rows,
    adapters_here,
    ids_ref,
    slots_ref,
    weight_ref,
    down_ref,
    up_ref,
    weight_out,
    down_out,
    up_out,
    holds_out,
    sems,
):
    blocks, rank, _ = down_out.shape
    base = lax.axis_index("wide") * adapters_here
    copies = [pltpu.make_async_copy(weight_ref, weight_out, sems.at[2 * blocks])]
    for block in range(blocks):
        adapter = jnp.clip(ids_ref[block] - base, 0, adapters_here - 1)
        copies.append(
            pltpu.make_async_copy(down_ref.at[adapter], down_out.at[block], sems.at[2 * block])
        )
        copies.append(
            pltpu.make_async_copy(up_ref.at[adapter], up_out.at[block], sems.at[2 * block + 1])
        )
    for copy in copies:
        copy.start()
    requests = holds_out.shape[0]
    line = lax.broadcasted_iota(jnp.int32, (requests, rank), 0)
    place, within = line // rows, line % rows
    device = place
    for index, member in enumerate(order):
        if member != index:
            device = jnp.where(place == index, member, device)
    request = device * rows + within
    for block in range(blocks):
        held = request == slots_ref[block, 0]
        for slot in range(1, slots_ref.shape[1]):
            held = held | (request == slots_ref[block, slot])
        holds_out[:, block * rank : (block + 1) * rank] = held.astype(jnp.float32)
    for copy in copies:
        copy.wait()


def project(own_columns_ref, other_columns_ref, weight_ref, projected_ref):
    feature_count, half_width = weight_ref.shape
    mine = lax.axis_index("wide") * feature_count // half_width == lax.axis_index("tp")
    columns = jnp.where(mine, own_columns_ref[...], other_columns_ref[...])
    projected_ref[...] = jnp.dot(columns, weight_ref[...], preferred_element_type=jnp.float32)


def combine(
    first, second, rows, projected_ref, own_ref, other_ref, holds_ref, up_ref, sent_ref
):
    inner = (own_ref[...] + other_ref[...]).astype(jnp.bfloat16)
    inner = jnp.where(holds_ref[...] != 0, inner, jnp.zeros_like(inner))
    total = projected_ref[...] + jnp.dot(inner, up_ref[...], preferred_element_type=jnp.float32)
    for place, device in enumerate(second):
        start = first.index(device) * rows
        sent_ref[place] = total[start : start + rows].astype(sent_ref.dtype)


def local(
    hidden,
    residual,
    output_weight,
    adapter_down_factor,
    adapter_up_factor,
    gain,
    block_request_rows,
    adapter_of_block,
):
    rows, width = hidden.shape
    half_width = residual.shape[1]
    wide = lax.axis_size("wide")
    requests = wide * rows
    feature_count = output_weight.shape[0]
    adapters_here, rank, _ = adapter_down_factor.shape
    blocks = adapter_of_block.shape[0]
    swap = [(0, 1), (1, 0)]
    first, second = exchange_orders(wide)

    params = pltpu.CompilerParams(vmem_limit_bytes=16 * 2**20)

    def exchange(sent, axes, groups):
        return lax.all_to_all(sent, axes, 0, 0, axis_index_groups=groups)

    groups = [
        [2 * device + (core_in_first_group(device, wide) + group) % 2 for device in first]
        for group in range(2)
    ]
    sent = pl.pallas_call(
        functools.partial(pack, first, half_width),
        out_shape=jax.ShapeDtypeStruct((wide, rows, half_width), jnp.bfloat16),
        in_specs=[VMEM],
        out_specs=VMEM,
        compiler_params=params,
        name="pack",
    )(*in_hbm(hidden))
    half_rows = exchange(sent, ("wide", "tp"), groups).reshape(requests, half_width)

    factor = (blocks, rank, half_width)
    weight, selected_down, selected_up, holds = pl.pallas_call(
        functools.partial(fetch, first, rows, adapters_here),
        out_shape=[pltpu.VMEM(output_weight.shape, jnp.bfloat16)]
        + [pltpu.VMEM(factor, jnp.bfloat16)] * 2
        + [pltpu.VMEM((requests, blocks * rank), jnp.float32)],
        in_specs=[SMEM, SMEM, HBM, HBM, HBM],
        out_specs=[VMEM] * 4,
        scratch_shapes=[pltpu.SemaphoreType.DMA((2 * blocks + 1,))],
        cost_estimate=pl.CostEstimate(
            flops=0, bytes_accessed=8 * blocks * rank * half_width, transcendentals=0
        ),
        compiler_params=params,
        name="fetch",
    )(
        *in_hbm(
            adapter_of_block,
            block_request_rows,
            output_weight,
            adapter_down_factor,
            adapter_up_factor,
        )
    )
    selected_down = selected_down.reshape(blocks * rank, half_width)
    selected_up = selected_up.reshape(blocks * rank, half_width)

    start = lax.axis_index("wide") * feature_count
    own_columns = lax.dynamic_slice_in_dim(half_rows, start % half_width, feature_count, 1)
    other_columns = lax.ppermute(own_columns, "tp", swap)
    inner_part = lax.dot_general(
        half_rows, selected_down, (((1,), (1,)), ((), ())), preferred_element_type=jnp.float32
    )
    inner_other = lax.ppermute(inner_part, "tp", swap)
    projected = pl.pallas_call(
        project,
        out_shape=pltpu.VMEM((requests, half_width), jnp.float32),
        in_specs=[VMEM] * 3,
        out_specs=VMEM,
        compiler_params=params,
        cost_estimate=pl.CostEstimate(
            flops=2 * requests * feature_count * half_width,
            bytes_accessed=2 * feature_count * half_width + 4 * requests * half_width,
            transcendentals=0,
        ),
        name="project",
    )(*in_vmem(own_columns, other_columns, weight))
    terms = pl.pallas_call(
        functools.partial(combine, first, second, rows),
        out_shape=pltpu.VMEM((wide, rows, half_width), jnp.bfloat16),
        in_specs=[VMEM] * 5,
        out_specs=VMEM,
        compiler_params=params,
        name="combine",
    )(*in_vmem(projected, inner_part, inner_other, holds, selected_up))
    terms = exchange(terms, "wide", [second])
    summed = residual.astype(jnp.float32) + jnp.sum(terms.astype(jnp.float32), axis=0)
    squares = jnp.sum(summed * summed, axis=1, keepdims=True)
    squares += lax.ppermute(squares, "tp", swap)
    normed = summed * lax.rsqrt(squares / width + epsilon) * gain
    return (summed.astype(jnp.bfloat16), normed.astype(jnp.bfloat16))


def solution(mesh):
    return jax.shard_map(
        local,
        mesh=mesh,
        in_specs=(
            P(("grp", "wide"), None),
            P(("grp", "wide"), "tp"),
            P("wide", "tp"),
            P("wide", None, "tp"),
            P("wide", None, "tp"),
            P("tp"),
            P(("grp", "wide"), None),
            P(("grp", "wide")),
        ),
        out_specs=(P(("grp", "wide"), "tp"), P(("grp", "wide"), "tp")),
        check_vma=False,
    )
```

```python
import functools

import jax
import jax.numpy as jnp
from jax import lax
from jax.experimental import pallas as pl
from jax.experimental.pallas import tpu as pltpu
from jax.sharding import PartitionSpec as P

epsilon = 1e-06
VMEM = pl.BlockSpec(memory_space=pltpu.VMEM)
SMEM = pl.BlockSpec(memory_space=pltpu.SMEM)
HBM = pl.BlockSpec(memory_space=pltpu.HBM)


def in_vmem(*arrays):
    return [pltpu.with_memory_space_constraint(array, pltpu.VMEM) for array in arrays]


def in_hbm(*arrays):
    return [pltpu.with_memory_space_constraint(array, pltpu.HBM) for array in arrays]


def exchange_orders(wide):
    if wide == 8:
        return [3, 4, 7, 0, 1, 6, 2, 5], [4, 6, 0, 7, 5, 1, 2, 3]
    middle = wide // 2
    order = [middle] + [index for index in range(wide) if index != middle]
    return order, order


def core_in_first_group(device, wide):
    return device // (wide // 2)


def pack(order, half_width, hidden_ref, sent_ref):
    wide = sent_ref.shape[0]
    core = lax.axis_index("tp")
    swapped = (core + core_in_first_group(lax.axis_index("wide"), wide)) % 2
    halves = []
    for member_core in range(2):
        start = pl.multiple_of((member_core + swapped) % 2 * half_width, 128)
        halves.append(hidden_ref[:, pl.ds(start, half_width)])
    for place, device in enumerate(order):
        sent_ref[place] = halves[core_in_first_group(device, wide)]


def fetch(
    order,
    rows,
    adapters_here,
    ids_ref,
    slots_ref,
    weight_ref,
    down_ref,
    up_ref,
    weight_out,
    down_out,
    up_out,
    holds_out,
    down_rows,
    sems,
):
    blocks, rank, _ = up_out.shape
    base = lax.axis_index("wide") * adapters_here
    copies = [pltpu.make_async_copy(weight_ref, weight_out, sems.at[2 * blocks])]
    for block in range(blocks):
        adapter = jnp.clip(ids_ref[block] - base, 0, adapters_here - 1)
        copies.append(
            pltpu.make_async_copy(down_ref.at[adapter], down_rows.at[block], sems.at[2 * block])
        )
        copies.append(
            pltpu.make_async_copy(up_ref.at[adapter], up_out.at[block], sems.at[2 * block + 1])
        )
    for copy in copies:
        copy.start()
    requests = holds_out.shape[0]
    line = lax.broadcasted_iota(jnp.int32, (requests, rank), 0)
    place, within = line // rows, line % rows
    device = place
    for index, member in enumerate(order):
        if member != index:
            device = jnp.where(place == index, member, device)
    request = device * rows + within
    for block in range(blocks):
        held = request == slots_ref[block, 0]
        for slot in range(1, slots_ref.shape[1]):
            held = held | (request == slots_ref[block, slot])
        holds_out[:, block * rank : (block + 1) * rank] = held.astype(jnp.float32)
    for copy in copies:
        copy.wait()
    for block in range(blocks):
        down_out[:, block * rank : (block + 1) * rank] = down_rows[block].T


def project(own_columns_ref, other_columns_ref, weight_ref, projected_ref):
    feature_count, half_width = weight_ref.shape
    mine = lax.axis_index("wide") * feature_count // half_width == lax.axis_index("tp")
    columns = jnp.where(mine, own_columns_ref[...], other_columns_ref[...])
    projected_ref[...] = jnp.dot(columns, weight_ref[...], preferred_element_type=jnp.float32)


def combine(
    first, second, rows, projected_ref, own_ref, other_ref, holds_ref, up_ref, sent_ref
):
    inner = (own_ref[...] + other_ref[...]).astype(jnp.bfloat16)
    inner = jnp.where(holds_ref[...] != 0, inner, jnp.zeros_like(inner))
    total = projected_ref[...] + jnp.dot(inner, up_ref[...], preferred_element_type=jnp.float32)
    for place, device in enumerate(second):
        start = first.index(device) * rows
        sent_ref[place] = total[start : start + rows].astype(sent_ref.dtype)


def local(
    hidden,
    residual,
    output_weight,
    adapter_down_factor,
    adapter_up_factor,
    gain,
    block_request_rows,
    adapter_of_block,
):
    rows, width = hidden.shape
    half_width = residual.shape[1]
    wide = lax.axis_size("wide")
    requests = wide * rows
    feature_count = output_weight.shape[0]
    adapters_here, rank, _ = adapter_down_factor.shape
    blocks = adapter_of_block.shape[0]
    swap = [(0, 1), (1, 0)]
    first, second = exchange_orders(wide)

    params = pltpu.CompilerParams(vmem_limit_bytes=16 * 2**20)

    def exchange(sent, axes, groups):
        return lax.all_to_all(sent, axes, 0, 0, axis_index_groups=groups)

    groups = [
        [2 * device + (core_in_first_group(device, wide) + group) % 2 for device in first]
        for group in range(2)
    ]
    sent = pl.pallas_call(
        functools.partial(pack, first, half_width),
        out_shape=jax.ShapeDtypeStruct((wide, rows, half_width), jnp.bfloat16),
        in_specs=[VMEM],
        out_specs=VMEM,
        compiler_params=params,
        name="pack",
    )(*in_hbm(hidden))
    half_rows = exchange(sent, ("wide", "tp"), groups).reshape(requests, half_width)

    factor = (blocks, rank, half_width)
    weight, selected_down, selected_up, holds = pl.pallas_call(
        functools.partial(fetch, first, rows, adapters_here),
        out_shape=[pltpu.VMEM(output_weight.shape, jnp.bfloat16)]
        + [pltpu.VMEM((half_width, blocks * rank), jnp.bfloat16), pltpu.VMEM(factor, jnp.bfloat16)]
        + [pltpu.VMEM((requests, blocks * rank), jnp.float32)],
        in_specs=[SMEM, SMEM, HBM, HBM, HBM],
        out_specs=[VMEM] * 4,
        scratch_shapes=[
            pltpu.VMEM(factor, jnp.bfloat16),
            pltpu.SemaphoreType.DMA((2 * blocks + 1,)),
        ],
        cost_estimate=pl.CostEstimate(
            flops=0, bytes_accessed=8 * blocks * rank * half_width, transcendentals=0
        ),
        compiler_params=params,
        name="fetch",
    )(
        *in_hbm(
            adapter_of_block,
            block_request_rows,
            output_weight,
            adapter_down_factor,
            adapter_up_factor,
        )
    )
    selected_up = selected_up.reshape(blocks * rank, half_width)

    start = lax.axis_index("wide") * feature_count
    own_columns = lax.dynamic_slice_in_dim(half_rows, start % half_width, feature_count, 1)
    other_columns = lax.ppermute(own_columns, "tp", swap)
    inner_part = jnp.dot(half_rows, selected_down, preferred_element_type=jnp.float32)
    inner_other = lax.ppermute(inner_part, "tp", swap)
    projected = pl.pallas_call(
        project,
        out_shape=pltpu.VMEM((requests, half_width), jnp.float32),
        in_specs=[VMEM] * 3,
        out_specs=VMEM,
        compiler_params=params,
        cost_estimate=pl.CostEstimate(
            flops=2 * requests * feature_count * half_width,
            bytes_accessed=2 * feature_count * half_width + 4 * requests * half_width,
            transcendentals=0,
        ),
        name="project",
    )(*in_vmem(own_columns, other_columns, weight))
    terms = pl.pallas_call(
        functools.partial(combine, first, second, rows),
        out_shape=pltpu.VMEM((wide, rows, half_width), jnp.bfloat16),
        in_specs=[VMEM] * 5,
        out_specs=VMEM,
        compiler_params=params,
        name="combine",
    )(*in_vmem(projected, inner_part, inner_other, holds, selected_up))
    terms = exchange(terms, "wide", [second])
    summed = residual.astype(jnp.float32) + jnp.sum(terms.astype(jnp.float32), axis=0)
    squares = jnp.sum(summed * summed, axis=1, keepdims=True)
    squares += lax.ppermute(squares, "tp", swap)
    normed = summed * lax.rsqrt(squares / width + epsilon) * gain
    return (summed.astype(jnp.bfloat16), normed.astype(jnp.bfloat16))


def solution(mesh):
    return jax.shard_map(
        local,
        mesh=mesh,
        in_specs=(
            P(("grp", "wide"), None),
            P(("grp", "wide"), "tp"),
            P("wide", "tp"),
            P("wide", None, "tp"),
            P("wide", None, "tp"),
            P("tp"),
            P(("grp", "wide"), None),
            P(("grp", "wide")),
        ),
        out_specs=(P(("grp", "wide"), "tp"), P(("grp", "wide"), "tp")),
        check_vma=False,
    )
```

```python
import functools

import jax
import jax.numpy as jnp
from jax import lax
from jax.experimental import pallas as pl
from jax.experimental.pallas import tpu as pltpu
from jax.sharding import PartitionSpec as P

epsilon = 1e-06
VMEM = pl.BlockSpec(memory_space=pltpu.VMEM)
SMEM = pl.BlockSpec(memory_space=pltpu.SMEM)
HBM = pl.BlockSpec(memory_space=pltpu.HBM)


def in_vmem(*arrays):
    return [pltpu.with_memory_space_constraint(array, pltpu.VMEM) for array in arrays]


def in_hbm(*arrays):
    return [pltpu.with_memory_space_constraint(array, pltpu.HBM) for array in arrays]


def exchange_orders(wide):
    if wide == 8:
        return [3, 2, 7, 0, 1, 6, 4, 5], [4, 6, 0, 7, 5, 1, 2, 3]
    middle = wide // 2
    order = [middle] + [index for index in range(wide) if index != middle]
    return order, order


def core_in_first_group(device, wide):
    return device // (wide // 2)


def pack(order, half_width, hidden_ref, sent_ref):
    wide = sent_ref.shape[0]
    core = lax.axis_index("tp")
    swapped = (core + core_in_first_group(lax.axis_index("wide"), wide)) % 2
    halves = []
    for member_core in range(2):
        start = pl.multiple_of((member_core + swapped) % 2 * half_width, 128)
        halves.append(hidden_ref[:, pl.ds(start, half_width)])
    for place, device in enumerate(order):
        sent_ref[place] = halves[core_in_first_group(device, wide)]


def fetch(
    order,
    rows,
    adapters_here,
    ids_ref,
    slots_ref,
    weight_ref,
    down_ref,
    up_ref,
    residual_ref,
    weight_out,
    down_out,
    up_out,
    holds_out,
    residual_out,
    sems,
):
    blocks, rank, _ = down_out.shape
    base = lax.axis_index("wide") * adapters_here
    copies = [pltpu.make_async_copy(weight_ref, weight_out, sems.at[2 * blocks])]
    for block in range(blocks):
        adapter = jnp.clip(ids_ref[block] - base, 0, adapters_here - 1)
        copies.append(
            pltpu.make_async_copy(down_ref.at[adapter], down_out.at[block], sems.at[2 * block])
        )
        copies.append(
            pltpu.make_async_copy(up_ref.at[adapter], up_out.at[block], sems.at[2 * block + 1])
        )
    for copy in copies:
        copy.start()
    residual_out[...] = residual_ref[...].astype(jnp.float32)
    requests = holds_out.shape[0]
    line = lax.broadcasted_iota(jnp.int32, (requests, rank), 0)
    place, within = line // rows, line % rows
    device = place
    for index, member in enumerate(order):
        if member != index:
            device = jnp.where(place == index, member, device)
    request = device * rows + within
    for block in range(blocks):
        held = request == slots_ref[block, 0]
        for slot in range(1, slots_ref.shape[1]):
            held = held | (request == slots_ref[block, slot])
        holds_out[:, block * rank : (block + 1) * rank] = held.astype(jnp.float32)
    for copy in copies:
        copy.wait()


def project(own_columns_ref, other_columns_ref, weight_ref, projected_ref):
    feature_count, half_width = weight_ref.shape
    mine = lax.axis_index("wide") * feature_count // half_width == lax.axis_index("tp")
    columns = jnp.where(mine, own_columns_ref[...], other_columns_ref[...])
    projected_ref[...] = jnp.dot(columns, weight_ref[...], preferred_element_type=jnp.float32)


def combine(
    first, second, rows, projected_ref, own_ref, other_ref, holds_ref, up_ref, sent_ref
):
    inner = (own_ref[...] + other_ref[...]).astype(jnp.bfloat16)
    inner = jnp.where(holds_ref[...] != 0, inner, jnp.zeros_like(inner))
    total = projected_ref[...] + jnp.dot(inner, up_ref[...], preferred_element_type=jnp.float32)
    for place, device in enumerate(second):
        start = first.index(device) * rows
        sent_ref[place] = total[start : start + rows].astype(sent_ref.dtype)


def home(terms_ref, residual_ref, summed_ref, squares_ref):
    summed = residual_ref[...]
    for place in range(terms_ref.shape[0]):
        summed += terms_ref[place].astype(jnp.float32)
    summed_ref[...] = summed
    squares = jnp.sum(summed * summed, axis=1, keepdims=True)
    squares_ref[...] = squares


def local(
    hidden,
    residual,
    output_weight,
    adapter_down_factor,
    adapter_up_factor,
    gain,
    block_request_rows,
    adapter_of_block,
):
    rows, width = hidden.shape
    half_width = residual.shape[1]
    wide = lax.axis_size("wide")
    requests = wide * rows
    feature_count = output_weight.shape[0]
    adapters_here, rank, _ = adapter_down_factor.shape
    blocks = adapter_of_block.shape[0]
    swap = [(0, 1), (1, 0)]
    first, second = exchange_orders(wide)

    params = pltpu.CompilerParams(vmem_limit_bytes=16 * 2**20)

    def exchange(sent, axes, groups):
        return lax.all_to_all(sent, axes, 0, 0, axis_index_groups=groups)

    groups = [
        [2 * device + (core_in_first_group(device, wide) + group) % 2 for device in first]
        for group in range(2)
    ]
    sent = pl.pallas_call(
        functools.partial(pack, first, half_width),
        out_shape=jax.ShapeDtypeStruct((wide, rows, half_width), jnp.bfloat16),
        in_specs=[VMEM],
        out_specs=VMEM,
        compiler_params=params,
        name="pack",
    )(*in_hbm(hidden))
    half_rows = exchange(sent, ("wide", "tp"), groups).reshape(requests, half_width)

    factor = (blocks, rank, half_width)
    weight, selected_down, selected_up, holds, residual_here = pl.pallas_call(
        functools.partial(fetch, first, rows, adapters_here),
        out_shape=[pltpu.VMEM(output_weight.shape, jnp.bfloat16)]
        + [pltpu.VMEM(factor, jnp.bfloat16)] * 2
        + [
            pltpu.VMEM((requests, blocks * rank), jnp.float32),
            pltpu.VMEM((rows, half_width), jnp.float32),
        ],
        in_specs=[SMEM, SMEM, HBM, HBM, HBM, VMEM],
        out_specs=[VMEM] * 5,
        scratch_shapes=[pltpu.SemaphoreType.DMA((2 * blocks + 1,))],
        cost_estimate=pl.CostEstimate(
            flops=0, bytes_accessed=8 * blocks * rank * half_width, transcendentals=0
        ),
        compiler_params=params,
        name="fetch",
    )(
        *in_hbm(
            adapter_of_block,
            block_request_rows,
            output_weight,
            adapter_down_factor,
            adapter_up_factor,
            residual,
        )
    )
    selected_down = selected_down.reshape(blocks * rank, half_width)
    selected_up = selected_up.reshape(blocks * rank, half_width)

    start = lax.axis_index("wide") * feature_count
    own_columns = lax.dynamic_slice_in_dim(half_rows, start % half_width, feature_count, 1)
    other_columns = lax.ppermute(own_columns, "tp", swap)
    inner_part = lax.dot_general(
        half_rows, selected_down, (((1,), (1,)), ((), ())), preferred_element_type=jnp.float32
    )
    inner_other = lax.ppermute(inner_part, "tp", swap)
    projected = pl.pallas_call(
        project,
        out_shape=pltpu.VMEM((requests, half_width), jnp.float32),
        in_specs=[VMEM] * 3,
        out_specs=VMEM,
        compiler_params=params,
        cost_estimate=pl.CostEstimate(
            flops=2 * requests * feature_count * half_width,
            bytes_accessed=2 * feature_count * half_width + 4 * requests * half_width,
            transcendentals=0,
        ),
        name="project",
    )(*in_vmem(own_columns, other_columns, weight))
    terms = pl.pallas_call(
        functools.partial(combine, first, second, rows),
        out_shape=pltpu.VMEM((wide, rows, half_width), jnp.bfloat16),
        in_specs=[VMEM] * 5,
        out_specs=VMEM,
        compiler_params=params,
        name="combine",
    )(*in_vmem(projected, inner_part, inner_other, holds, selected_up))
    terms = exchange(terms, "wide", [second])
    summed, squares = pl.pallas_call(
        home,
        out_shape=[
            pltpu.VMEM((rows, half_width), jnp.float32),
            pltpu.VMEM((rows, 1), jnp.float32),
        ],
        in_specs=[VMEM] * 2,
        out_specs=[VMEM] * 2,
        compiler_params=params,
        name="home",
    )(*in_vmem(terms, residual_here))
    squares += lax.ppermute(squares, "tp", swap)
    normed = summed * lax.rsqrt(squares / width + epsilon) * gain
    return (summed.astype(jnp.bfloat16), normed.astype(jnp.bfloat16))


def solution(mesh):
    return jax.shard_map(
        local,
        mesh=mesh,
        in_specs=(
            P(("grp", "wide"), None),
            P(("grp", "wide"), "tp"),
            P("wide", "tp"),
            P("wide", None, "tp"),
            P("wide", None, "tp"),
            P("tp"),
            P(("grp", "wide"), None),
            P(("grp", "wide")),
        ),
        out_specs=(P(("grp", "wide"), "tp"), P(("grp", "wide"), "tp")),
        check_vma=False,
    )
```

```python
import functools

import jax
import jax.numpy as jnp
from jax import lax
from jax.experimental import pallas as pl
from jax.experimental.pallas import tpu as pltpu
from jax.sharding import PartitionSpec as P

epsilon = 1e-06
VMEM = pl.BlockSpec(memory_space=pltpu.VMEM)
SMEM = pl.BlockSpec(memory_space=pltpu.SMEM)
HBM = pl.BlockSpec(memory_space=pltpu.HBM)


def in_vmem(*arrays):
    return [pltpu.with_memory_space_constraint(array, pltpu.VMEM) for array in arrays]


def in_hbm(*arrays):
    return [pltpu.with_memory_space_constraint(array, pltpu.HBM) for array in arrays]


def exchange_orders(wide):
    if wide == 8:
        return [3, 2, 7, 0, 1, 6, 4, 5], [4, 6, 0, 7, 5, 1, 2, 3]
    middle = wide // 2
    order = [middle] + [index for index in range(wide) if index != middle]
    return order, order


def core_in_first_group(device, wide):
    return device // (wide // 2)


def pack(order, half_width, hidden_ref, sent_ref):
    wide = sent_ref.shape[0]
    core = lax.axis_index("tp")
    swapped = (core + core_in_first_group(lax.axis_index("wide"), wide)) % 2
    halves = []
    for member_core in range(2):
        start = pl.multiple_of((member_core + swapped) % 2 * half_width, 128)
        halves.append(hidden_ref[:, pl.ds(start, half_width)])
    for place, device in enumerate(order):
        sent_ref[place] = halves[core_in_first_group(device, wide)]


def fetch(
    order,
    rows,
    adapters_here,
    ids_ref,
    slots_ref,
    weight_ref,
    down_ref,
    up_ref,
    weight_out,
    down_out,
    up_out,
    holds_out,
    sems,
):
    blocks, rank, _ = down_out.shape
    base = lax.axis_index("wide") * adapters_here
    copies = [pltpu.make_async_copy(weight_ref, weight_out, sems.at[2 * blocks])]
    for block in range(blocks):
        adapter = jnp.clip(ids_ref[block] - base, 0, adapters_here - 1)
        copies.append(
            pltpu.make_async_copy(down_ref.at[adapter], down_out.at[block], sems.at[2 * block])
        )
        copies.append(
            pltpu.make_async_copy(up_ref.at[adapter], up_out.at[block], sems.at[2 * block + 1])
        )
    for copy in copies:
        copy.start()
    requests = holds_out.shape[0]
    line = lax.broadcasted_iota(jnp.int32, (requests, rank), 0)
    place, within = line // rows, line % rows
    device = place
    for index, member in enumerate(order):
        if member != index:
            device = jnp.where(place == index, member, device)
    request = device * rows + within
    for block in range(blocks):
        held = request == slots_ref[block, 0]
        for slot in range(1, slots_ref.shape[1]):
            held = held | (request == slots_ref[block, slot])
        holds_out[:, block * rank : (block + 1) * rank] = held.astype(jnp.float32)
    for copy in copies:
        copy.wait()


def project(own_columns_ref, other_columns_ref, weight_ref, projected_ref):
    feature_count, half_width = weight_ref.shape
    mine = lax.axis_index("wide") * feature_count // half_width == lax.axis_index("tp")
    columns = jnp.where(mine, own_columns_ref[...], other_columns_ref[...])
    projected_ref[...] = jnp.dot(columns, weight_ref[...], preferred_element_type=jnp.float32)


def combine(
    first, second, rows, projected_ref, own_ref, other_ref, holds_ref, up_ref, sent_ref
):
    inner = (own_ref[...] + other_ref[...]).astype(jnp.bfloat16)
    inner = jnp.where(holds_ref[...] != 0, inner, jnp.zeros_like(inner))
    total = projected_ref[...] + jnp.dot(inner, up_ref[...], preferred_element_type=jnp.float32)
    for place, device in enumerate(second):
        start = first.index(device) * rows
        sent_ref[place] = total[start : start + rows].astype(sent_ref.dtype)


def local(
    hidden,
    residual,
    output_weight,
    adapter_down_factor,
    adapter_up_factor,
    gain,
    block_request_rows,
    adapter_of_block,
):
    rows, width = hidden.shape
    half_width = residual.shape[1]
    wide = lax.axis_size("wide")
    requests = wide * rows
    feature_count = output_weight.shape[0]
    adapters_here, rank, _ = adapter_down_factor.shape
    blocks = adapter_of_block.shape[0]
    swap = [(0, 1), (1, 0)]
    first, second = exchange_orders(wide)

    params = pltpu.CompilerParams(vmem_limit_bytes=16 * 2**20)

    def exchange(sent, axes, groups):
        return lax.all_to_all(sent, axes, 0, 0, axis_index_groups=groups)

    groups = [
        [2 * device + (core_in_first_group(device, wide) + group) % 2 for device in first]
        for group in range(2)
    ]
    sent = pl.pallas_call(
        functools.partial(pack, first, half_width),
        out_shape=jax.ShapeDtypeStruct((wide, rows, half_width), jnp.bfloat16),
        in_specs=[VMEM],
        out_specs=VMEM,
        compiler_params=params,
        name="pack",
    )(*in_hbm(hidden))
    received = exchange(sent, ("wide", "tp"), groups)
    half_rows = received.reshape(requests, half_width)

    factor = (blocks, rank, half_width)
    weight, selected_down, selected_up, holds = pl.pallas_call(
        functools.partial(fetch, first, rows, adapters_here),
        out_shape=[pltpu.VMEM(output_weight.shape, jnp.bfloat16)]
        + [pltpu.VMEM(factor, jnp.bfloat16)] * 2
        + [pltpu.VMEM((requests, blocks * rank), jnp.float32)],
        in_specs=[SMEM, SMEM, HBM, HBM, HBM],
        out_specs=[VMEM] * 4,
        scratch_shapes=[pltpu.SemaphoreType.DMA((2 * blocks + 1,))],
        cost_estimate=pl.CostEstimate(
            flops=0, bytes_accessed=8 * blocks * rank * half_width, transcendentals=0
        ),
        compiler_params=params,
        name="fetch",
    )(
        *in_hbm(
            adapter_of_block,
            block_request_rows,
            output_weight,
            adapter_down_factor,
            adapter_up_factor,
        )
    )
    selected_down = selected_down.reshape(blocks * rank, half_width)
    selected_up = selected_up.reshape(blocks * rank, half_width)

    start = lax.axis_index("wide") * feature_count
    own_columns = lax.dynamic_slice_in_dim(received, start % half_width, feature_count, 2)
    other_columns = lax.ppermute(own_columns, "tp", swap).reshape(requests, feature_count)
    own_columns = own_columns.reshape(requests, feature_count)
    inner_part = lax.dot_general(
        half_rows, selected_down, (((1,), (1,)), ((), ())), preferred_element_type=jnp.float32
    )
    inner_other = lax.ppermute(inner_part, "tp", swap)
    projected = pl.pallas_call(
        project,
        out_shape=pltpu.VMEM((requests, half_width), jnp.float32),
        in_specs=[VMEM] * 3,
        out_specs=VMEM,
        compiler_params=params,
        cost_estimate=pl.CostEstimate(
            flops=2 * requests * feature_count * half_width,
            bytes_accessed=2 * feature_count * half_width + 4 * requests * half_width,
            transcendentals=0,
        ),
        name="project",
    )(*in_vmem(own_columns, other_columns, weight))
    terms = pl.pallas_call(
        functools.partial(combine, first, second, rows),
        out_shape=pltpu.VMEM((wide, rows, half_width), jnp.bfloat16),
        in_specs=[VMEM] * 5,
        out_specs=VMEM,
        compiler_params=params,
        name="combine",
    )(*in_vmem(projected, inner_part, inner_other, holds, selected_up))
    terms = exchange(terms, "wide", [second])
    summed = residual.astype(jnp.float32) + jnp.sum(terms.astype(jnp.float32), axis=0)
    squares = jnp.sum(summed * summed, axis=1, keepdims=True)
    squares += lax.ppermute(squares, "tp", swap)
    normed = summed * lax.rsqrt(squares / width + epsilon) * gain
    return (summed.astype(jnp.bfloat16), normed.astype(jnp.bfloat16))


def solution(mesh):
    return jax.shard_map(
        local,
        mesh=mesh,
        in_specs=(
            P(("grp", "wide"), None),
            P(("grp", "wide"), "tp"),
            P("wide", "tp"),
            P("wide", None, "tp"),
            P("wide", None, "tp"),
            P("tp"),
            P(("grp", "wide"), None),
            P(("grp", "wide")),
        ),
        out_specs=(P(("grp", "wide"), "tp"), P(("grp", "wide"), "tp")),
        check_vma=False,
    )
```
